32 devices in a mesh: tau: 2 (over x), row: 16 (over z, y, core).
Axes of the slice: x: 2, y: 2, z: 4, core: 2. Of those that a mesh axis runs over, the one named last changes fastest.
Arguments:
- integrals: bfloat16 [2048, 3, 3, 4096], P('row'), may hold values from -0.3125 to 0.3125
- occupied: bfloat16 [32, 3, 64, 64], P('tau'), parts along dimension 0, may hold values from -0.4375 to 0.4375
- virtual: bfloat16 [32, 3, 64, 64], P('tau'), parts along dimension 0, may hold values from -0.4375 to 0.4375
- tile_mask: int32 [16, 3, 3], replicated, may hold values 0 or 1
Outputs:
- response: float32 [4096, 640], P(('tau', 'row')), parts along dimension 0
The draws below stay inside these ranges and needn't reach their ends.
There are 2 independent parts, one for each index of `tau`. The reference program is written for one: setup_inputs(seed, part) draws one part's arguments, and reference() takes and returns one part's arrays. A program takes and returns all parts, laid end to end along the dimension named above; an argument that names none is the same for every part. Nothing has to cross between parts.
All inputs are finite; a program needn't handle non-finite values.
Results may differ from the reference program's by a relative error of at most 0.0041.
Values may be sent and summed in bfloat16 or wider, within the bound.
A program may use at most 128 MiB of HBM per device.

```python
import jax
import jax.numpy as jnp
from jax import lax

A = 64
R = 128
J = 3
NBAND = 3
NAB = 16
NRI = 2048
NQ = 640


def with_ends(result, stream_key, least, largest):
    longest = result.shape.index(max(result.shape))
    spots = []
    for shift in (0, 1):
        where = [jax.random.randint(jax.random.fold_in(stream_key, axis), (), 0, length) for axis, length in enumerate(result.shape)]
        where[longest] = (where[longest] + shift) % result.shape[longest]
        spots.append(tuple(where))
    return result.at[spots[0]].set(least).at[spots[1]].set(largest)


def levels(rng, dims, cuts, least, largest):
    def one(position, shards_of):
        heights = jax.random.uniform(jax.random.fold_in(jax.random.fold_in(rng, 6), position), (shards_of,), jnp.float32, least / len(cuts), largest / len(cuts))
        return jnp.repeat(jnp.exp(heights), dims[position] // shards_of).reshape((-1,) + (1,) * (len(dims) - position - 1))

    loudness = one(*cuts[0])
    for cut in cuts[1:]:
        loudness = loudness * one(*cut)
    return loudness


def scatter_about(stream_key, dims, scale, bound, shards=(), kind=jnp.bfloat16):
    factor_of = levels(stream_key, dims, shards, -0.22, 0.18) if shards else 1.0
    result = jax.random.normal(stream_key, dims, jnp.float32) * scale * factor_of
    return jnp.minimum(jnp.maximum(result, -bound), bound).astype(kind)


def setup_inputs(seed: int = 0, part: int = 0) -> dict:
    key_list = jax.random.split(jax.random.key(seed), 5)
    own_keys = jax.random.split(jax.random.fold_in(key_list[4], part), 5)
    return {
        "integrals": scatter_about(key_list[0], (NRI, J, NBAND, A * A), (2 * J * A) ** -0.5, 0.3125, ((0, 16),)),
        "occupied": scatter_about(own_keys[1], (NAB, NBAND, A, A), (NBAND * A) ** -0.5, 0.4375),
        "virtual": scatter_about(own_keys[2], (NAB, NBAND, A, A), (NBAND * A) ** -0.5, 0.4375),
        "tile_mask": with_ends((jax.random.randint(key_list[3], (NAB, J, NBAND), 0, 4) < 3).astype(jnp.int32), jax.random.fold_in(key_list[3], 1), 0, 1),
    }


def reference(integrals, occupied, virtual, tile_mask):
    reach = J // 2
    middle = NBAND // 2
    tiles = integrals.reshape(NAB, R, J, NBAND, A, A)
    gates = tile_mask.astype(integrals.dtype)

    def masked_block(block):
        index = (block % NAB).astype(jnp.int32)
        raw = jnp.take(tiles, index, axis=0)
        gate = jnp.take(gates, index, axis=0)
        return raw * gate[None, :, :, None, None]

    def one_block(carry, block):
        own = masked_block(block).astype(jnp.float32)
        occ_near = jnp.take(occupied, (block - reach + jnp.arange(J, dtype=jnp.int32)) % NAB, axis=0).astype(jnp.float32)
        vir_near = jnp.take(virtual, (block - reach - middle + jnp.arange(J + NBAND - 1, dtype=jnp.int32)) % NAB, axis=0).astype(jnp.float32)
        products = []
        for column in range(J):
            row_tiles = []
            for band in range(NBAND):
                summed = jnp.zeros((R, A, A), jnp.float32)
                for inner in range(J):
                    offset = column - inner + band
                    second = column - inner + middle
                    if 0 <= offset < NBAND and 0 <= second < NBAND:
                        summed = summed + jnp.einsum("puv,vl->pul", own[:, inner, offset], occ_near[inner, second])
                row_tiles.append(summed.astype(jnp.bfloat16))
            products.append(row_tiles)
        virt_part = []
        for column in range(J):
            row_tiles = []
            for sigma in range(NBAND):
                summed = jnp.zeros((R, A, A), jnp.float32)
                for band in range(NBAND):
                    second = band - sigma + middle
                    if 0 <= second < NBAND:
                        summed = summed + jnp.einsum("su,pul->psl", vir_near[column + sigma, second], products[column][band].astype(jnp.float32))
                row_tiles.append(summed.astype(jnp.bfloat16))
            virt_part.append(row_tiles)
        panels = []
        for near in range(2 * J - 1):
            other = masked_block(block + near - 2 * reach).astype(jnp.float32)
            summed = jnp.zeros((R, R), jnp.float32)
            for column in range(J):
                partner = column - near + 2 * reach
                if 0 <= partner < J:
                    for sigma in range(NBAND):
                        summed = summed + jnp.einsum("psl,qsl->pq", virt_part[column][sigma].astype(jnp.float32), other[:, partner, sigma])
            panels.append(summed)
        return carry, jnp.concatenate(panels, axis=1)

    unused, rows = lax.scan(one_block, jnp.zeros((), jnp.float32), jnp.arange(NAB, dtype=jnp.int32))
    return -2.0 * rows.reshape(NRI, NQ)
```

```python
import functools

import jax
import jax.numpy as jnp
from jax import lax
from jax.experimental import pallas as pl
from jax.experimental.pallas import tpu as pltpu
from jax.sharding import PartitionSpec as P

F32 = jnp.float32
BF16 = jnp.bfloat16
MESH = pl.DeviceIdType.MESH
NB_TILES = 5
OWN_TERMS = (((0, 1), (1, 3)), ((0, 2), (1, 4), (2, 6)), ((1, 5), (2, 7)))


def kernel(
    tau_count, row_count, width,
    tiles_ref, weight_ref, virt_ref, gate_ref,
    out_ref,
    own, near, prod, part, virt, panels, sending, arriving, total,
    own_sem, inner_send, inner_recv, outer_send, outer_recv, fwd_send, fwd_recv, end_send, end_recv,
):
    rows = own.shape[1]
    square = own.shape[2]
    tau = lax.axis_index("tau")
    me = lax.axis_index("row")
    odd = lax.rem(me, 2)
    inner = me + 1 - 2 * odd
    outer = lax.rem(me - 1 + 2 * odd + row_count, row_count)
    share = rows // tau_count
    first = pl.multiple_of(tau * share, share)

    barrier = pltpu.get_barrier_semaphore()
    pl.semaphore_signal(barrier, inc=1, device_id={"row": inner}, device_id_type=MESH)
    pl.semaphore_signal(barrier, inc=1, device_id={"row": outer}, device_id_type=MESH)
    for step in range(1, tau_count):
        pl.semaphore_signal(
            barrier, inc=1, device_id={"tau": lax.rem(tau + step, tau_count)}, device_id_type=MESH
        )
    pl.semaphore_wait(barrier, tau_count + 1)

    outer_copies = []
    for t in range(NB_TILES):
        copy = pltpu.make_async_remote_copy(
            src_ref=tiles_ref.at[4 * odd + t, pl.ds(first, share)],
            dst_ref=near.at[1, t, pl.ds(first, share)],
            send_sem=outer_send.at[t], recv_sem=outer_recv.at[t],
            device_id={"row": outer}, device_id_type=MESH,
        )
        copy.start()
        outer_copies.append(copy)
    own_copy = pltpu.make_async_copy(tiles_ref, own, own_sem)
    own_copy.start()
    inner_copies = []
    for t in range(NB_TILES):
        copy = pltpu.make_async_remote_copy(
            src_ref=tiles_ref.at[4 * (1 - odd) + t],
            dst_ref=near.at[0, t],
            send_sem=inner_send.at[t], recv_sem=inner_recv.at[t],
            device_id={"row": inner}, device_id_type=MESH,
        )
        copy.start()
        inner_copies.append(copy)

    fwd_copies = []

    def forward(t):
        outer_copies[t].wait_recv()
        for step in range(1, tau_count):
            place = near.at[1, t, pl.ds(first, share)]
            copy = pltpu.make_async_remote_copy(
                src_ref=place, dst_ref=place,
                send_sem=fwd_send.at[t, step - 1], recv_sem=fwd_recv.at[t, step - 1],
                device_id={"tau": lax.rem(tau + step, tau_count)}, device_id_type=MESH,
            )
            copy.start()
            fwd_copies.append(copy)

    def products(load, base, terms):
        def at(step, carry):
            lane = pl.multiple_of(step * 256, 256)
            for o in range(3):
                halves = []
                for half in range(2):
                    halves.append(jnp.concatenate(
                        [load(t, pl.ds(lane + 128 * half, 128)) for unused, t in terms[o]], axis=1))
                weight = jnp.concatenate([weight_ref[base + k, o] for k, unused in terms[o]], axis=1)
                result = lax.dot_general(
                    weight, jnp.concatenate(halves, axis=0), (((1,), (1,)), ((), ())),
                    preferred_element_type=F32)
                prod[o, pl.ds(lane, 128), :] = result[:, :rows]
                prod[o, pl.ds(lane + 128, 128), :] = result[:, rows:]
            return carry

        lax.fori_loop(0, square // 256, at, 0)

    def virtual(block):
        def at(step, carry):
            columns = []
            for half in range(2):
                columns.append(jnp.concatenate(
                    [prod[m, pl.ds(2 * step + half, width, stride=width), :] for m in range(3)], axis=0))
            right = jnp.concatenate(columns, axis=1).astype(BF16)
            result = jnp.dot(virt_ref[...], right, preferred_element_type=F32)
            for half in range(2):
                for m in range(3):
                    part[m, pl.ds(2 * step + half, width, stride=width), :] = result[
                        m * width:(m + 1) * width, half * rows:(half + 1) * rows]
            return carry

        lax.fori_loop(0, width // 2, at, 0)

        def rounded(step, carry):
            place = pl.ds(pl.multiple_of(step * 512, 512), 512)
            for m in range(3):
                virt[m, place, block * rows:(block + 1) * rows] = part[m, place, :].astype(BF16)
            return carry

        lax.fori_loop(0, square // 512, rounded, 0)

    def panel(load, slot, low, high):
        result = None
        for m in range(3):
            def at(step, carry, m=m):
                place = pl.ds(pl.multiple_of(step * 512, 512), 512)
                return carry + jnp.dot(
                    load(m, place), virt[m, place, low * rows:high * rows],
                    preferred_element_type=F32)

            term = lax.fori_loop(
                0, square // 512, at, jnp.zeros((rows, (high - low) * rows), F32))
            term = term * gate_ref[slot, m]
            result = term if result is None else result + term
        panels[slot, :, low * rows:high * rows] = result

    def near_load(slot):
        return lambda t, lanes: near[slot, t, :, lanes]

    def near_partner(slot, offset):
        return lambda m, lanes: near[slot, offset + m, :, lanes]

    def own_load(t, lanes):
        return own[t, :, lanes]

    def own_partner(m, lanes):
        return own[3 + m, :, lanes]

    near_terms = tuple(((0, o), (1, 2 + o)) for o in range(3))

    own_copy.wait()
    products(own_load, 0, OWN_TERMS)
    virtual(0)
    forward(0)
    panel(own_partner, 0, 0, 1)
    for copy in inner_copies:
        copy.wait_recv()
    products(near_load(0), 3, near_terms)
    forward(1)
    virtual(1)
    panel(near_partner(0, 2 * odd), 1, 0, 2)
    panel(own_partner, 0, 1, 2)
    for t in range(2, NB_TILES):
        forward(t)
    for copy in fwd_copies:
        copy.wait_recv()
    products(near_load(1), 5, near_terms)
    virtual(2)
    panel(near_partner(1, 2 * (1 - odd)), 2, 0, 3)
    panel(own_partner, 0, 2, 3)
    panel(near_partner(0, 2 * odd), 1, 2, 3)

    places = (1, 2 * (1 - odd), 2 * odd)
    for block in (1, 2):
        for slot in range(3):
            sending[block - 1, places[slot]] = panels[slot, :, block * rows:(block + 1) * rows].T
    end_copies = []
    for block, target in ((1, inner), (2, outer)):
        copy = pltpu.make_async_remote_copy(
            src_ref=sending.at[block - 1], dst_ref=arriving.at[block - 1],
            send_sem=end_send.at[block - 1], recv_sem=end_recv.at[block - 1],
            device_id={"row": target}, device_id_type=MESH,
        )
        copy.start()
        end_copies.append(copy)
    total[0] = jnp.zeros((rows, rows), F32)
    total[4] = jnp.zeros((rows, rows), F32)
    for slot in range(3):
        total[1 + places[slot]] = panels[slot, :, :rows].T
    for index, place in ((0, 2 * (1 - odd)), (1, 2 * odd)):
        end_copies[index].wait_recv()
        for k in range(3):
            total[place + k] += arriving[index, k]
    for c in range(5):
        out_ref[:, c * rows:(c + 1) * rows] = total[c] * -2.0
    for copy in outer_copies + inner_copies + fwd_copies + end_copies:
        copy.wait_send()


def per_device(tau_count, row_count, integrals, occupied, virtual, tile_mask):
    rows, col_count, band_count, square = integrals.shape
    width = occupied.shape[-1]
    blocks = occupied.shape[0]
    n = lax.axis_index("row")
    odd = lax.rem(n, 2)
    tiles = integrals.transpose(1, 2, 0, 3).reshape(col_count * band_count, rows, square)

    around = (n - 1 + jnp.arange(3, dtype=jnp.int32)) % blocks
    occ = jnp.take(occupied, around, axis=0)
    vir = jnp.take(virtual, around, axis=0)
    flags = jnp.take(tile_mask, around, axis=0).reshape(3, 9)
    scale = flags.astype(BF16)

    own_w = jnp.stack([
        scale[1, 1:4, None, None] * occ[0, 2],
        scale[1, 3:6, None, None] * occ[1, 1],
        scale[1, 5:8, None, None] * occ[2, 0],
    ])
    keep_high = jnp.array([0, 1, 1], BF16)
    keep_low = jnp.array([1, 1, 0], BF16)
    right_w = jnp.stack([
        scale[2, 0:3, None, None] * occ[1, 1],
        (keep_high * scale[2, 2:5])[:, None, None] * occ[2, 0],
    ])
    left_w = jnp.stack([
        (keep_low * scale[0, 4:7])[:, None, None] * occ[0, 2],
        scale[0, 6:9, None, None] * occ[1, 1],
    ])
    inner_w = jnp.where(odd == 0, right_w, left_w)
    outer_w = jnp.where(odd == 0, left_w, right_w)
    small = jnp.swapaxes(jnp.concatenate([own_w, inner_w, outer_w]), 2, 3)
    eye = jnp.eye(2, dtype=BF16)
    weight = (small[:, :, None, :, None, :] * eye[None, None, :, None, :, None]).reshape(
        7, 3, 2 * width, 2 * width)

    zero = jnp.zeros((width, width), BF16)
    vmat = jnp.block([
        [vir[a, b - a + 1] if 0 <= b - a + 1 < 3 else zero for b in range(3)] for a in range(3)
    ])
    right_gate, left_gate = flags[2, 0:3], flags[0, 6:9]
    gates = jnp.stack([
        flags[1, 3:6],
        jnp.where(odd == 0, right_gate, left_gate),
        jnp.where(odd == 0, left_gate, right_gate),
    ]).astype(F32)

    vmem = pl.BlockSpec(memory_space=pltpu.VMEM)
    dma = pltpu.SemaphoreType.DMA
    return pl.pallas_call(
        functools.partial(kernel, tau_count, row_count, width),
        out_shape=jax.ShapeDtypeStruct((rows, 5 * rows), F32),
        in_specs=[
            pl.BlockSpec(memory_space=pl.ANY), vmem, vmem,
            pl.BlockSpec(memory_space=pltpu.SMEM),
        ],
        out_specs=vmem,
        scratch_shapes=[
            pltpu.VMEM((9, rows, square), BF16),
            pltpu.VMEM((2, NB_TILES, rows, square), BF16),
            pltpu.VMEM((3, square, rows), F32),
            pltpu.VMEM((3, square, rows), F32),
            pltpu.VMEM((3, square, 3 * rows), BF16),
            pltpu.VMEM((3, rows, 3 * rows), F32),
            pltpu.VMEM((2, 3, rows, rows), F32),
            pltpu.VMEM((2, 3, rows, rows), F32),
            pltpu.VMEM((5, rows, rows), F32),
            dma, dma((NB_TILES,)), dma((NB_TILES,)), dma((NB_TILES,)), dma((NB_TILES,)),
            dma((NB_TILES, max(1, tau_count - 1))), dma((NB_TILES, max(1, tau_count - 1))),
            dma((2,)), dma((2,)),
        ],
        compiler_params=pltpu.CompilerParams(
            collective_id=0, has_side_effects=True, vmem_limit_bytes=56 * 1024 * 1024),
    )(tiles, weight, vmat, gates)


def solution(mesh):
    in_specs = (
        P("row", None, None, None),
        P("tau", None, None, None),
        P("tau", None, None, None),
        P(),
    )
    out_specs = P(("tau", "row"), None)
    return jax.shard_map(
        functools.partial(per_device, mesh.shape["tau"], mesh.shape["row"]),
        mesh=mesh, in_specs=in_specs, out_specs=out_specs, check_vma=False,
    )
```

```python
import functools

import jax
import jax.numpy as jnp
from jax import lax
from jax.experimental import pallas as pl
from jax.experimental.pallas import tpu as pltpu
from jax.sharding import PartitionSpec as P

F32 = jnp.float32
BF16 = jnp.bfloat16
MESH = pl.DeviceIdType.MESH
NB_TILES = 5
OWN_TERMS = (((0, 1), (1, 3)), ((0, 2), (1, 4), (2, 6)), ((1, 5), (2, 7)))


def kernel(
    tau_count, row_count, width,
    tiles_ref, weight_ref, virt_ref, gate_ref,
    out_ref,
    own, near, prod, part, virt, panels, sending, arriving, total,
    own_sem, inner_send, inner_recv, outer_send, outer_recv, fwd_send, fwd_recv, end_send, end_recv,
):
    rows = own.shape[1]
    square = own.shape[2]
    tau = lax.axis_index("tau")
    me = lax.axis_index("row")
    odd = lax.rem(me, 2)
    inner = me + 1 - 2 * odd
    outer = lax.rem(me - 1 + 2 * odd + row_count, row_count)
    share = rows // tau_count
    first = pl.multiple_of(tau * share, share)

    barrier = pltpu.get_barrier_semaphore()
    pl.semaphore_signal(barrier, inc=1, device_id={"row": inner}, device_id_type=MESH)
    pl.semaphore_signal(barrier, inc=1, device_id={"row": outer}, device_id_type=MESH)
    for step in range(1, tau_count):
        pl.semaphore_signal(
            barrier, inc=1, device_id={"tau": lax.rem(tau + step, tau_count)}, device_id_type=MESH
        )
    pl.semaphore_wait(barrier, tau_count + 1)

    outer_copies = []
    for t in range(NB_TILES):
        copy = pltpu.make_async_remote_copy(
            src_ref=tiles_ref.at[4 * odd + t, pl.ds(first, share)],
            dst_ref=near.at[1, t, pl.ds(first, share)],
            send_sem=outer_send.at[t], recv_sem=outer_recv.at[t],
            device_id={"row": outer}, device_id_type=MESH,
        )
        copy.start()
        outer_copies.append(copy)
    own_copy = pltpu.make_async_copy(tiles_ref, own, own_sem)
    own_copy.start()
    inner_copies = []
    for t in range(NB_TILES):
        copy = pltpu.make_async_remote_copy(
            src_ref=tiles_ref.at[4 * (1 - odd) + t],
            dst_ref=near.at[0, t],
            send_sem=inner_send.at[t], recv_sem=inner_recv.at[t],
            device_id={"row": inner}, device_id_type=MESH,
        )
        copy.start()
        inner_copies.append(copy)

    fwd_copies = []

    def forward(t):
        outer_copies[t].wait_recv()
        for step in range(1, tau_count):
            place = near.at[1, t, pl.ds(first, share)]
            copy = pltpu.make_async_remote_copy(
                src_ref=place, dst_ref=place,
                send_sem=fwd_send.at[t, step - 1], recv_sem=fwd_recv.at[t, step - 1],
                device_id={"tau": lax.rem(tau + step, tau_count)}, device_id_type=MESH,
            )
            copy.start()
            fwd_copies.append(copy)

    def products(load, base, terms):
        def at(step, carry):
            lane = pl.multiple_of(step * 256, 256)
            for o in range(3):
                halves = []
                for half in range(2):
                    halves.append(jnp.concatenate(
                        [load(t, pl.ds(lane + 128 * half, 128)) for unused, t in terms[o]], axis=1))
                weight = jnp.concatenate([weight_ref[base + k, o] for k, unused in terms[o]], axis=1)
                result = lax.dot_general(
                    weight, jnp.concatenate(halves, axis=0), (((1,), (1,)), ((), ())),
                    preferred_element_type=F32)
                prod[o, pl.ds(lane, 128), :] = result[:, :rows]
                prod[o, pl.ds(lane + 128, 128), :] = result[:, rows:]
            return carry

        lax.fori_loop(0, square // 256, at, 0, unroll=4)

    def virtual(block):
        def at(step, carry):
            columns = []
            for half in range(2):
                columns.append(jnp.concatenate(
                    [prod[m, pl.ds(2 * step + half, width, stride=width), :] for m in range(3)], axis=0))
            right = jnp.concatenate(columns, axis=1).astype(BF16)
            result = jnp.dot(virt_ref[...], right, preferred_element_type=F32)
            for half in range(2):
                for m in range(3):
                    part[m, pl.ds(2 * step + half, width, stride=width), :] = result[
                        m * width:(m + 1) * width, half * rows:(half + 1) * rows]
            return carry

        lax.fori_loop(0, width // 2, at, 0, unroll=4)

        def rounded(step, carry):
            place = pl.ds(pl.multiple_of(step * 512, 512), 512)
            for m in range(3):
                virt[m, place, block * rows:(block + 1) * rows] = part[m, place, :].astype(BF16)
            return carry

        lax.fori_loop(0, square // 512, rounded, 0, unroll=2)

    def panel(load, slot, low, high):
        result = None
        for m in range(3):
            def at(step, carry, m=m):
                place = pl.ds(pl.multiple_of(step * 512, 512), 512)
                return carry + jnp.dot(
                    load(m, place), virt[m, place, low * rows:high * rows],
                    preferred_element_type=F32)

            term = lax.fori_loop(
                0, square // 512, at, jnp.zeros((rows, (high - low) * rows), F32), unroll=4)
            term = term * gate_ref[slot, m]
            result = term if result is None else result + term
        panels[slot, :, low * rows:high * rows] = result

    def near_load(slot):
        return lambda t, lanes: near[slot, t, :, lanes]

    def near_partner(slot, offset):
        return lambda m, lanes: near[slot, offset + m, :, lanes]

    def own_load(t, lanes):
        return own[t, :, lanes]

    def own_partner(m, lanes):
        return own[3 + m, :, lanes]

    near_terms = tuple(((0, o), (1, 2 + o)) for o in range(3))

    own_copy.wait()
    products(own_load, 0, OWN_TERMS)
    virtual(0)
    forward(0)
    panel(own_partner, 0, 0, 1)
    for copy in inner_copies:
        copy.wait_recv()
    products(near_load(0), 3, near_terms)
    forward(1)
    virtual(1)
    panel(near_partner(0, 2 * odd), 1, 0, 2)
    panel(own_partner, 0, 1, 2)
    for t in range(2, NB_TILES):
        forward(t)
    for copy in fwd_copies:
        copy.wait_recv()
    products(near_load(1), 5, near_terms)
    virtual(2)
    panel(near_partner(1, 2 * (1 - odd)), 2, 0, 3)
    panel(own_partner, 0, 2, 3)
    panel(near_partner(0, 2 * odd), 1, 2, 3)

    places = (1, 2 * (1 - odd), 2 * odd)
    for block in (1, 2):
        for slot in range(3):
            sending[block - 1, places[slot]] = panels[slot, :, block * rows:(block + 1) * rows].T
    end_copies = []
    for block, target in ((1, inner), (2, outer)):
        copy = pltpu.make_async_remote_copy(
            src_ref=sending.at[block - 1], dst_ref=arriving.at[block - 1],
            send_sem=end_send.at[block - 1], recv_sem=end_recv.at[block - 1],
            device_id={"row": target}, device_id_type=MESH,
        )
        copy.start()
        end_copies.append(copy)
    total[0] = jnp.zeros((rows, rows), F32)
    total[4] = jnp.zeros((rows, rows), F32)
    for slot in range(3):
        total[1 + places[slot]] = panels[slot, :, :rows].T
    for index, place in ((0, 2 * (1 - odd)), (1, 2 * odd)):
        end_copies[index].wait_recv()
        for k in range(3):
            total[place + k] += arriving[index, k]
    for c in range(5):
        out_ref[:, c * rows:(c + 1) * rows] = total[c] * -2.0
    for copy in outer_copies + inner_copies + fwd_copies + end_copies:
        copy.wait_send()


def per_device(tau_count, row_count, integrals, occupied, virtual, tile_mask):
    rows, col_count, band_count, square = integrals.shape
    width = occupied.shape[-1]
    blocks = occupied.shape[0]
    n = lax.axis_index("row")
    odd = lax.rem(n, 2)
    tiles = integrals.transpose(1, 2, 0, 3).reshape(col_count * band_count, rows, square)

    around = (n - 1 + jnp.arange(3, dtype=jnp.int32)) % blocks
    occ = jnp.take(occupied, around, axis=0)
    vir = jnp.take(virtual, around, axis=0)
    flags = jnp.take(tile_mask, around, axis=0).reshape(3, 9)
    scale = flags.astype(BF16)

    own_w = jnp.stack([
        scale[1, 1:4, None, None] * occ[0, 2],
        scale[1, 3:6, None, None] * occ[1, 1],
        scale[1, 5:8, None, None] * occ[2, 0],
    ])
    keep_high = jnp.array([0, 1, 1], BF16)
    keep_low = jnp.array([1, 1, 0], BF16)
    right_w = jnp.stack([
        scale[2, 0:3, None, None] * occ[1, 1],
        (keep_high * scale[2, 2:5])[:, None, None] * occ[2, 0],
    ])
    left_w = jnp.stack([
        (keep_low * scale[0, 4:7])[:, None, None] * occ[0, 2],
        scale[0, 6:9, None, None] * occ[1, 1],
    ])
    inner_w = jnp.where(odd == 0, right_w, left_w)
    outer_w = jnp.where(odd == 0, left_w, right_w)
    small = jnp.swapaxes(jnp.concatenate([own_w, inner_w, outer_w]), 2, 3)
    eye = jnp.eye(2, dtype=BF16)
    weight = (small[:, :, None, :, None, :] * eye[None, None, :, None, :, None]).reshape(
        7, 3, 2 * width, 2 * width)

    zero = jnp.zeros((width, width), BF16)
    vmat = jnp.block([
        [vir[a, b - a + 1] if 0 <= b - a + 1 < 3 else zero for b in range(3)] for a in range(3)
    ])
    right_gate, left_gate = flags[2, 0:3], flags[0, 6:9]
    gates = jnp.stack([
        flags[1, 3:6],
        jnp.where(odd == 0, right_gate, left_gate),
        jnp.where(odd == 0, left_gate, right_gate),
    ]).astype(F32)

    vmem = pl.BlockSpec(memory_space=pltpu.VMEM)
    dma = pltpu.SemaphoreType.DMA
    return pl.pallas_call(
        functools.partial(kernel, tau_count, row_count, width),
        out_shape=jax.ShapeDtypeStruct((rows, 5 * rows), F32),
        in_specs=[
            pl.BlockSpec(memory_space=pl.ANY), vmem, vmem,
            pl.BlockSpec(memory_space=pltpu.SMEM),
        ],
        out_specs=vmem,
        scratch_shapes=[
            pltpu.VMEM((9, rows, square), BF16),
            pltpu.VMEM((2, NB_TILES, rows, square), BF16),
            pltpu.VMEM((3, square, rows), F32),
            pltpu.VMEM((3, square, rows), F32),
            pltpu.VMEM((3, square, 3 * rows), BF16),
            pltpu.VMEM((3, rows, 3 * rows), F32),
            pltpu.VMEM((2, 3, rows, rows), F32),
            pltpu.VMEM((2, 3, rows, rows), F32),
            pltpu.VMEM((5, rows, rows), F32),
            dma, dma((NB_TILES,)), dma((NB_TILES,)), dma((NB_TILES,)), dma((NB_TILES,)),
            dma((NB_TILES, max(1, tau_count - 1))), dma((NB_TILES, max(1, tau_count - 1))),
            dma((2,)), dma((2,)),
        ],
        compiler_params=pltpu.CompilerParams(
            collective_id=0, has_side_effects=True, vmem_limit_bytes=56 * 1024 * 1024),
    )(tiles, weight, vmat, gates)


def solution(mesh):
    in_specs = (
        P("row", None, None, None),
        P("tau", None, None, None),
        P("tau", None, None, None),
        P(),
    )
    out_specs = P(("tau", "row"), None)
    return jax.shard_map(
        functools.partial(per_device, mesh.shape["tau"], mesh.shape["row"]),
        mesh=mesh, in_specs=in_specs, out_specs=out_specs, check_vma=False,
    )
```

```python
import functools

import jax
import jax.numpy as jnp
from jax import lax
from jax.experimental import pallas as pl
from jax.experimental.pallas import tpu as pltpu
from jax.sharding import PartitionSpec as P

F32 = jnp.float32
BF16 = jnp.bfloat16
MESH = pl.DeviceIdType.MESH
NB_TILES = 5
ORDER = (0, 2, 1, 3, 4)
OWN_TERMS = (((0, 1), (1, 3)), ((0, 2), (1, 4), (2, 6)), ((1, 5), (2, 7)))


def kernel(
    tau_count, row_count, width,
    tiles_ref, occ_ref, vir_ref, mask_ref,
    out_ref,
    weight_ref, virt_ref, own, near, prod, part, virt, panels, sending, arriving, total,
    own_sem, inner_send, inner_recv, outer_send, outer_recv, fwd_send, fwd_recv, end_send, end_recv,
):
    rows = own.shape[1]
    square = own.shape[2]
    tau = lax.axis_index("tau")
    me = lax.axis_index("row")
    odd = lax.rem(me, 2)
    inner = me + 1 - 2 * odd
    outer = lax.rem(me - 1 + 2 * odd + row_count, row_count)
    share = rows // tau_count
    first = pl.multiple_of(tau * share, share)

    barrier = pltpu.get_barrier_semaphore()
    pl.semaphore_signal(barrier, inc=1, device_id={"row": inner}, device_id_type=MESH)
    pl.semaphore_signal(barrier, inc=1, device_id={"row": outer}, device_id_type=MESH)
    for step in range(1, tau_count):
        pl.semaphore_signal(
            barrier, inc=1, device_id={"tau": lax.rem(tau + step, tau_count)}, device_id_type=MESH
        )
    pl.semaphore_wait(barrier, tau_count + 1)

    outer_copies = {}
    for t in ORDER:
        copy = pltpu.make_async_remote_copy(
            src_ref=tiles_ref.at[4 * odd + t, pl.ds(first, share)],
            dst_ref=near.at[1, t, pl.ds(first, share)],
            send_sem=outer_send.at[t], recv_sem=outer_recv.at[t],
            device_id={"row": outer}, device_id_type=MESH,
        )
        copy.start()
        outer_copies[t] = copy
    own_copy = pltpu.make_async_copy(tiles_ref, own, own_sem)
    own_copy.start()
    inner_copies = []
    for t in range(NB_TILES):
        copy = pltpu.make_async_remote_copy(
            src_ref=tiles_ref.at[4 * (1 - odd) + t],
            dst_ref=near.at[0, t],
            send_sem=inner_send.at[t], recv_sem=inner_recv.at[t],
            device_id={"row": inner}, device_id_type=MESH,
        )
        copy.start()
        inner_copies.append(copy)

    fwd_copies = {t: [] for t in ORDER}

    def forward(t):
        outer_copies[t].wait_recv()
        for step in range(1, tau_count):
            place = near.at[1, t, pl.ds(first, share)]
            copy = pltpu.make_async_remote_copy(
                src_ref=place, dst_ref=place,
                send_sem=fwd_send.at[t, step - 1], recv_sem=fwd_recv.at[t, step - 1],
                device_id={"tau": lax.rem(tau + step, tau_count)}, device_id_type=MESH,
            )
            copy.start()
            fwd_copies[t].append(copy)

    left = lax.rem(me - 1 + row_count, row_count)
    right = lax.rem(me + 1, row_count)
    inner_kind = (1 - odd).astype(F32)
    outer_kind = odd.astype(F32)

    def flag(block, tile):
        return mask_ref[block, tile // 3, tile % 3].astype(F32)

    def setup():
        def spread(block):
            turned = block.T
            blank = jnp.zeros((width, width), F32)
            return jnp.concatenate([
                jnp.concatenate([turned, blank], axis=1),
                jnp.concatenate([blank, turned], axis=1),
            ], axis=0)

        before = spread(occ_ref[left, 2].astype(F32))
        middle = spread(occ_ref[me, 1].astype(F32))
        after = spread(occ_ref[right, 0].astype(F32))
        for o in range(3):
            for k, (matrix, tile) in enumerate(((before, 1 + o), (middle, 3 + o), (after, 5 + o))):
                weight_ref[k, o] = (matrix * flag(me, tile)).astype(BF16)
            for base, kind in ((3, inner_kind), (5, outer_kind)):
                other = 1.0 - kind
                first_right = kind * flag(right, o)
                second_right = kind * flag(right, 2 + o) if o > 0 else 0.0
                first_left = other * flag(left, 4 + o) if o < 2 else 0.0
                second_left = other * flag(left, 6 + o)
                weight_ref[base, o] = (middle * first_right + before * first_left).astype(BF16)
                weight_ref[base + 1, o] = (after * second_right + middle * second_left).astype(BF16)
        owners = (left, me, right)
        blank = jnp.zeros((width, width), F32)
        for a in range(3):
            virt_ref[a * width:(a + 1) * width, :] = jnp.concatenate([
                vir_ref[owners[a], b - a + 1].astype(F32) if 0 <= b - a + 1 < 3 else blank
                for b in range(3)
            ], axis=1).astype(BF16)

    def gate(slot, m):
        if slot == 0:
            return flag(me, 3 + m)
        kind = inner_kind if slot == 1 else outer_kind
        return kind * flag(right, m) + (1.0 - kind) * flag(left, 6 + m)

    def products(load, base, terms, bands=(0, 1, 2)):
        def at(step, carry):
            lane = pl.multiple_of(step * 256, 256)
            for o in bands:
                halves = []
                for half in range(2):
                    halves.append(jnp.concatenate(
                        [load(t, pl.ds(lane + 128 * half, 128)) for unused, t in terms[o]], axis=1))
                weight = jnp.concatenate([weight_ref[base + k, o] for k, unused in terms[o]], axis=1)
                result = lax.dot_general(
                    weight, jnp.concatenate(halves, axis=0), (((1,), (1,)), ((), ())),
                    preferred_element_type=F32)
                prod[o, pl.ds(lane, 128), :] = result[:, :rows]
                prod[o, pl.ds(lane + 128, 128), :] = result[:, rows:]
            return carry

        lax.fori_loop(0, square // 256, at, 0, unroll=4)

    def virtual(block):
        def at(step, carry):
            columns = []
            for half in range(2):
                columns.append(jnp.concatenate(
                    [prod[m, pl.ds(2 * step + half, width, stride=width), :] for m in range(3)], axis=0))
            right = jnp.concatenate(columns, axis=1).astype(BF16)
            result = jnp.dot(virt_ref[...], right, preferred_element_type=F32)
            for half in range(2):
                for m in range(3):
                    part[m, pl.ds(2 * step + half, width, stride=width), :] = result[
                        m * width:(m + 1) * width, half * rows:(half + 1) * rows]
            return carry

        lax.fori_loop(0, width // 2, at, 0, unroll=4)

        def rounded(step, carry):
            place = pl.ds(pl.multiple_of(step * 512, 512), 512)
            for m in range(3):
                virt[m, place, block * rows:(block + 1) * rows] = part[m, place, :].astype(BF16)
            return carry

        lax.fori_loop(0, square // 512, rounded, 0, unroll=2)

    def panel(load, slot, low, high):
        result = None
        for m in range(3):
            def at(step, carry, m=m):
                place = pl.ds(pl.multiple_of(step * 512, 512), 512)
                return carry + jnp.dot(
                    load(m, place), virt[m, place, low * rows:high * rows],
                    preferred_element_type=F32)

            term = lax.fori_loop(
                0, square // 512, at, jnp.zeros((rows, (high - low) * rows), F32), unroll=4)
            term = term * gate(slot, m)
            result = term if result is None else result + term
        panels[slot, :, low * rows:high * rows] = result

    def near_load(slot):
        return lambda t, lanes: near[slot, t, :, lanes]

    def near_partner(slot, offset):
        return lambda m, lanes: near[slot, offset + m, :, lanes]

    def own_load(t, lanes):
        return own[t, :, lanes]

    def own_partner(m, lanes):
        return own[3 + m, :, lanes]

    near_terms = tuple(((0, o), (1, 2 + o)) for o in range(3))

    def arrived(t):
        for copy in fwd_copies[t]:
            copy.wait_recv()

    setup()
    own_copy.wait()
    products(own_load, 0, OWN_TERMS)
    virtual(0)
    forward(0)
    panel(own_partner, 0, 0, 1)
    for copy in inner_copies:
        copy.wait_recv()
    products(near_load(0), 3, near_terms)
    forward(2)
    virtual(1)
    panel(near_partner(0, 2 * odd), 1, 0, 2)
    panel(own_partner, 0, 1, 2)
    forward(1)
    arrived(0)
    arrived(2)
    products(near_load(1), 5, near_terms, (0,))
    forward(3)
    arrived(1)
    arrived(3)
    products(near_load(1), 5, near_terms, (1,))
    forward(4)
    arrived(4)
    products(near_load(1), 5, near_terms, (2,))
    virtual(2)

    places = (1, 2 * (1 - odd), 2 * odd)
    end_copies = []

    def finish(block, slot, target):
        sending[block - 1, slot] = panels[slot, :, block * rows:(block + 1) * rows].T
        copy = pltpu.make_async_remote_copy(
            src_ref=sending.at[block - 1, slot], dst_ref=arriving.at[block - 1, places[slot]],
            send_sem=end_send.at[block - 1, slot], recv_sem=end_recv.at[block - 1, slot],
            device_id={"row": target}, device_id_type=MESH,
        )
        copy.start()
        end_copies.append(copy)

    panel(own_partner, 0, 2, 3)
    finish(2, 0, outer)
    panel(near_partner(0, 2 * odd), 1, 2, 3)
    finish(2, 1, outer)
    panel(near_partner(1, 2 * (1 - odd)), 2, 0, 3)
    finish(2, 2, outer)
    for slot in range(3):
        finish(1, slot, inner)
    total[0] = jnp.zeros((rows, rows), F32)
    total[4] = jnp.zeros((rows, rows), F32)
    for slot in range(3):
        total[1 + places[slot]] = panels[slot, :, :rows].T
    for copy in end_copies:
        copy.wait_recv()
    for index, place in ((0, 2 * (1 - odd)), (1, 2 * odd)):
        for k in range(3):
            total[place + k] += arriving[index, k]
    for c in range(5):
        out_ref[:, c * rows:(c + 1) * rows] = total[c] * -2.0
    for copy in list(outer_copies.values()) + inner_copies + end_copies:
        copy.wait_send()
    for group in fwd_copies.values():
        for copy in group:
            copy.wait_send()


def per_device(tau_count, row_count, integrals, occupied, virtual, tile_mask):
    rows, col_count, band_count, square = integrals.shape
    width = occupied.shape[-1]
    tiles = integrals.transpose(1, 2, 0, 3).reshape(col_count * band_count, rows, square)

    vmem = pl.BlockSpec(memory_space=pltpu.VMEM)
    dma = pltpu.SemaphoreType.DMA
    return pl.pallas_call(
        functools.partial(kernel, tau_count, row_count, width),
        out_shape=jax.ShapeDtypeStruct((rows, 5 * rows), F32),
        in_specs=[
            pl.BlockSpec(memory_space=pl.ANY), vmem, vmem,
            pl.BlockSpec(memory_space=pltpu.SMEM),
        ],
        out_specs=vmem,
        scratch_shapes=[
            pltpu.VMEM((7, 3, 2 * width, 2 * width), BF16),
            pltpu.VMEM((3 * width, 3 * width), BF16),
            pltpu.VMEM((9, rows, square), BF16),
            pltpu.VMEM((2, NB_TILES, rows, square), BF16),
            pltpu.VMEM((3, square, rows), F32),
            pltpu.VMEM((3, square, rows), F32),
            pltpu.VMEM((3, square, 3 * rows), BF16),
            pltpu.VMEM((3, rows, 3 * rows), F32),
            pltpu.VMEM((2, 3, rows, rows), F32),
            pltpu.VMEM((2, 3, rows, rows), F32),
            pltpu.VMEM((5, rows, rows), F32),
            dma, dma((NB_TILES,)), dma((NB_TILES,)), dma((NB_TILES,)), dma((NB_TILES,)),
            dma((NB_TILES, max(1, tau_count - 1))), dma((NB_TILES, max(1, tau_count - 1))),
            dma((2, 3)), dma((2, 3)),
        ],
        compiler_params=pltpu.CompilerParams(
            collective_id=0, has_side_effects=True, vmem_limit_bytes=56 * 1024 * 1024),
    )(tiles, occupied, virtual, tile_mask)


def solution(mesh):
    in_specs = (
        P("row", None, None, None),
        P("tau", None, None, None),
        P("tau", None, None, None),
        P(),
    )
    out_specs = P(("tau", "row"), None)
    return jax.shard_map(
        functools.partial(per_device, mesh.shape["tau"], mesh.shape["row"]),
        mesh=mesh, in_specs=in_specs, out_specs=out_specs, check_vma=False,
    )
```

```python
import functools

import jax
import jax.numpy as jnp
from jax import lax
from jax.experimental import pallas as pl
from jax.experimental.pallas import tpu as pltpu
from jax.sharding import PartitionSpec as P

F32 = jnp.float32
BF16 = jnp.bfloat16
MESH = pl.DeviceIdType.MESH
NB_TILES = 5
ORDER = (0, 2, 1, 3, 4)
OWN_TERMS = (((0, 1), (1, 3)), ((0, 2), (1, 4), (2, 6)), ((1, 5), (2, 7)))


def kernel(
    tau_count, row_count, width,
    tiles_ref, occ_ref, vir_ref, mask_ref,
    out_ref,
    weight_ref, virt_ref, own, near, prod, part, virt, panels, sending, arriving, total,
    own_sem, inner_send, inner_recv, outer_send, outer_recv, fwd_send, fwd_recv, end_send, end_recv,
):
    rows = own.shape[1]
    square = own.shape[2]
    pitch = prod.shape[1] // width
    tau = lax.axis_index("tau")
    me = lax.axis_index("row")
    odd = lax.rem(me, 2)
    inner = me + 1 - 2 * odd
    outer = lax.rem(me - 1 + 2 * odd + row_count, row_count)
    share = rows // tau_count
    first = pl.multiple_of(tau * share, share)

    barrier = pltpu.get_barrier_semaphore()
    pl.semaphore_signal(barrier, inc=1, device_id={"row": inner}, device_id_type=MESH)
    pl.semaphore_signal(barrier, inc=1, device_id={"row": outer}, device_id_type=MESH)
    for step in range(1, tau_count):
        pl.semaphore_signal(
            barrier, inc=1, device_id={"tau": lax.rem(tau + step, tau_count)}, device_id_type=MESH
        )
    pl.semaphore_wait(barrier, tau_count + 1)

    outer_copies = {}
    for t in ORDER:
        copy = pltpu.make_async_remote_copy(
            src_ref=tiles_ref.at[4 * odd + t, pl.ds(first, share)],
            dst_ref=near.at[1, t, pl.ds(first, share)],
            send_sem=outer_send.at[t], recv_sem=outer_recv.at[t],
            device_id={"row": outer}, device_id_type=MESH,
        )
        copy.start()
        outer_copies[t] = copy
    own_copy = pltpu.make_async_copy(tiles_ref, own, own_sem)
    own_copy.start()
    inner_copies = []
    for t in range(NB_TILES):
        copy = pltpu.make_async_remote_copy(
            src_ref=tiles_ref.at[4 * (1 - odd) + t],
            dst_ref=near.at[0, t],
            send_sem=inner_send.at[t], recv_sem=inner_recv.at[t],
            device_id={"row": inner}, device_id_type=MESH,
        )
        copy.start()
        inner_copies.append(copy)

    fwd_copies = {t: [] for t in ORDER}

    def forward(t):
        outer_copies[t].wait_recv()
        for step in range(1, tau_count):
            place = near.at[1, t, pl.ds(first, share)]
            copy = pltpu.make_async_remote_copy(
                src_ref=place, dst_ref=place,
                send_sem=fwd_send.at[t, step - 1], recv_sem=fwd_recv.at[t, step - 1],
                device_id={"tau": lax.rem(tau + step, tau_count)}, device_id_type=MESH,
            )
            copy.start()
            fwd_copies[t].append(copy)

    left = lax.rem(me - 1 + row_count, row_count)
    right = lax.rem(me + 1, row_count)
    inner_kind = (1 - odd).astype(F32)
    outer_kind = odd.astype(F32)

    def flag(block, tile):
        return mask_ref[block, tile // 3, tile % 3].astype(F32)

    def setup():
        def spread(block):
            turned = block.T
            blank = jnp.zeros((width, width), F32)
            return jnp.concatenate([
                jnp.concatenate([turned, blank], axis=1),
                jnp.concatenate([blank, turned], axis=1),
            ], axis=0)

        before = spread(occ_ref[left, 2].astype(F32))
        middle = spread(occ_ref[me, 1].astype(F32))
        after = spread(occ_ref[right, 0].astype(F32))
        for o in range(3):
            for k, (matrix, tile) in enumerate(((before, 1 + o), (middle, 3 + o), (after, 5 + o))):
                weight_ref[k, o] = (matrix * flag(me, tile)).astype(BF16)
            for base, kind in ((3, inner_kind), (5, outer_kind)):
                other = 1.0 - kind
                first_right = kind * flag(right, o)
                second_right = kind * flag(right, 2 + o) if o > 0 else 0.0
                first_left = other * flag(left, 4 + o) if o < 2 else 0.0
                second_left = other * flag(left, 6 + o)
                weight_ref[base, o] = (middle * first_right + before * first_left).astype(BF16)
                weight_ref[base + 1, o] = (after * second_right + middle * second_left).astype(BF16)
        owners = (left, me, right)
        blank = jnp.zeros((width, width), F32)
        for a in range(3):
            virt_ref[a * width:(a + 1) * width, :] = jnp.concatenate([
                vir_ref[owners[a], b - a + 1].astype(F32) if 0 <= b - a + 1 < 3 else blank
                for b in range(3)
            ], axis=1).astype(BF16)

    def gate(slot, m):
        if slot == 0:
            return flag(me, 3 + m)
        kind = inner_kind if slot == 1 else outer_kind
        return kind * flag(right, m) + (1.0 - kind) * flag(left, 6 + m)

    def products(load, base, terms, bands=(0, 1, 2)):
        def at(step, carry):
            lane = pl.multiple_of(step * 256, 256)
            for o in bands:
                halves = []
                for half in range(2):
                    halves.append(jnp.concatenate(
                        [load(t, pl.ds(lane + 128 * half, 128)) for unused, t in terms[o]], axis=1))
                weight = jnp.concatenate([weight_ref[base + k, o] for k, unused in terms[o]], axis=1)
                result = lax.dot_general(
                    weight, jnp.concatenate(halves, axis=0), (((1,), (1,)), ((), ())),
                    preferred_element_type=F32)
                for q in range(4):
                    place = pl.ds(pl.multiple_of((4 * step + q) * pitch, 8), width)
                    prod[o, place, :] = result[
                        (q % 2) * width:(q % 2 + 1) * width, (q // 2) * rows:(q // 2 + 1) * rows]
            return carry

        lax.fori_loop(0, square // 256, at, 0, unroll=4)

    def virtual(block):
        def at(step, carry):
            columns = []
            for half in range(2):
                columns.append(jnp.concatenate(
                    [prod[m, pl.ds(2 * step + half, width, stride=pitch), :] for m in range(3)], axis=0))
            right = jnp.concatenate(columns, axis=1).astype(BF16)
            result = jnp.dot(virt_ref[...], right, preferred_element_type=F32)
            for half in range(2):
                for m in range(3):
                    part[m, pl.ds(2 * step + half, width, stride=pitch), :] = result[
                        m * width:(m + 1) * width, half * rows:(half + 1) * rows]
            return carry

        lax.fori_loop(0, width // 2, at, 0, unroll=4)

        def rounded(step, carry):
            place = pl.ds(pl.multiple_of(step * 512, 512), 512)
            for m in range(3):
                virt[m, place, block * rows:(block + 1) * rows] = jnp.concatenate([
                    part[m, pl.ds(pl.multiple_of((8 * step + q) * pitch, 8), width), :]
                    for q in range(8)
                ], axis=0).astype(BF16)
            return carry

        lax.fori_loop(0, square // 512, rounded, 0, unroll=2)

    def panel(load, slot, low, high, bands=(0, 1, 2), more=False):
        result = panels[slot, :, low * rows:high * rows] if more else None
        for m in bands:
            def at(step, carry, m=m):
                place = pl.ds(pl.multiple_of(step * 512, 512), 512)
                return carry + jnp.dot(
                    load(m, place), virt[m, place, low * rows:high * rows],
                    preferred_element_type=F32)

            term = lax.fori_loop(
                0, square // 512, at, jnp.zeros((rows, (high - low) * rows), F32), unroll=4)
            term = term * gate(slot, m)
            result = term if result is None else result + term
        panels[slot, :, low * rows:high * rows] = result

    def near_load(slot):
        return lambda t, lanes: near[slot, t, :, lanes]

    def near_partner(slot, offset):
        return lambda m, lanes: near[slot, offset + m, :, lanes]

    def own_load(t, lanes):
        return own[t, :, lanes]

    def own_partner(m, lanes):
        return own[3 + m, :, lanes]

    near_terms = tuple(((0, o), (1, 2 + o)) for o in range(3))

    def arrived(t):
        for copy in fwd_copies[t]:
            copy.wait_recv()

    setup()
    own_copy.wait()
    products(own_load, 0, OWN_TERMS)
    virtual(0)
    forward(0)
    panel(own_partner, 0, 0, 1)
    for copy in inner_copies:
        copy.wait_recv()
    products(near_load(0), 3, near_terms)
    forward(2)
    virtual(1)
    panel(near_partner(0, 2 * odd), 1, 0, 2)
    panel(own_partner, 0, 1, 2)
    forward(1)
    arrived(0)
    arrived(2)
    products(near_load(1), 5, near_terms, (0,))
    forward(3)
    arrived(1)
    forward(4)
    arrived(3)
    products(near_load(1), 5, near_terms, (1,))
    panel(near_partner(1, 2 * (1 - odd)), 2, 0, 2, (0, 1))
    arrived(4)
    products(near_load(1), 5, near_terms, (2,))
    virtual(2)

    places = (1, 2 * (1 - odd), 2 * odd)
    end_copies = []

    def finish(block, slot, target):
        sending[block - 1, slot] = panels[slot, :, block * rows:(block + 1) * rows].T
        copy = pltpu.make_async_remote_copy(
            src_ref=sending.at[block - 1, slot], dst_ref=arriving.at[block - 1, places[slot]],
            send_sem=end_send.at[block - 1, slot], recv_sem=end_recv.at[block - 1, slot],
            device_id={"row": target}, device_id_type=MESH,
        )
        copy.start()
        end_copies.append(copy)

    panel(own_partner, 0, 2, 3)
    finish(2, 0, outer)
    panel(near_partner(0, 2 * odd), 1, 2, 3)
    finish(2, 1, outer)
    panel(near_partner(1, 2 * (1 - odd)), 2, 2, 3)
    finish(2, 2, outer)
    panel(near_partner(1, 2 * (1 - odd)), 2, 0, 2, (2,), True)
    for slot in range(3):
        finish(1, slot, inner)
    total[0] = jnp.zeros((rows, rows), F32)
    total[4] = jnp.zeros((rows, rows), F32)
    for slot in range(3):
        total[1 + places[slot]] = panels[slot, :, :rows].T
    for copy in end_copies:
        copy.wait_recv()
    for index, place in ((0, 2 * (1 - odd)), (1, 2 * odd)):
        for k in range(3):
            total[place + k] += arriving[index, k]
    for c in range(5):
        out_ref[:, c * rows:(c + 1) * rows] = total[c] * -2.0
    for copy in list(outer_copies.values()) + inner_copies + end_copies:
        copy.wait_send()
    for group in fwd_copies.values():
        for copy in group:
            copy.wait_send()


def per_device(tau_count, row_count, integrals, occupied, virtual, tile_mask):
    rows, col_count, band_count, square = integrals.shape
    width = occupied.shape[-1]
    tiles = integrals.transpose(1, 2, 0, 3).reshape(col_count * band_count, rows, square)

    vmem = pl.BlockSpec(memory_space=pltpu.VMEM)
    dma = pltpu.SemaphoreType.DMA
    return pl.pallas_call(
        functools.partial(kernel, tau_count, row_count, width),
        out_shape=jax.ShapeDtypeStruct((rows, 5 * rows), F32),
        in_specs=[
            pl.BlockSpec(memory_space=pl.ANY), vmem, vmem,
            pl.BlockSpec(memory_space=pltpu.SMEM),
        ],
        out_specs=vmem,
        scratch_shapes=[
            pltpu.VMEM((7, 3, 2 * width, 2 * width), BF16),
            pltpu.VMEM((3 * width, 3 * width), BF16),
            pltpu.VMEM((9, rows, square), BF16),
            pltpu.VMEM((2, NB_TILES, rows, square), BF16),
            pltpu.VMEM((3, square + 8 * width, rows), F32),
            pltpu.VMEM((3, square + 8 * width, rows), F32),
            pltpu.VMEM((3, square, 3 * rows), BF16),
            pltpu.VMEM((3, rows, 3 * rows), F32),
            pltpu.VMEM((2, 3, rows, rows), F32),
            pltpu.VMEM((2, 3, rows, rows), F32),
            pltpu.VMEM((5, rows, rows), F32),
            dma, dma((NB_TILES,)), dma((NB_TILES,)), dma((NB_TILES,)), dma((NB_TILES,)),
            dma((NB_TILES, max(1, tau_count - 1))), dma((NB_TILES, max(1, tau_count - 1))),
            dma((2, 3)), dma((2, 3)),
        ],
        compiler_params=pltpu.CompilerParams(
            collective_id=0, has_side_effects=True, vmem_limit_bytes=56 * 1024 * 1024),
    )(tiles, occupied, virtual, tile_mask)


def solution(mesh):
    in_specs = (
        P("row", None, None, None),
        P("tau", None, None, None),
        P("tau", None, None, None),
        P(),
    )
    out_specs = P(("tau", "row"), None)
    return jax.shard_map(
        functools.partial(per_device, mesh.shape["tau"], mesh.shape["row"]),
        mesh=mesh, in_specs=in_specs, out_specs=out_specs, check_vma=False,
    )
```

```python
import functools

import jax
import jax.numpy as jnp
from jax import lax
from jax.experimental import pallas as pl
from jax.experimental.pallas import tpu as pltpu
from jax.sharding import PartitionSpec as P

F32 = jnp.float32
BF16 = jnp.bfloat16
MESH = pl.DeviceIdType.MESH
NB_TILES = 5
ORDER = (0, 2, 1, 3, 4)
OWN_TERMS = (((0, 1), (1, 3)), ((0, 2), (1, 4), (2, 6)), ((1, 5), (2, 7)))


def kernel(
    tau_count, row_count, width,
    tiles_ref, occ_ref, vir_ref, mask_ref,
    out_ref,
    weight_ref, virt_ref, own, near, prod, part, virt, panels, sending, arriving, total,
    own_sem, inner_send, inner_recv, outer_send, outer_recv, fwd_send, fwd_recv, end_send, end_recv,
):
    rows = own.shape[1]
    square = own.shape[2]
    pitch = prod.shape[1] // width
    tau = lax.axis_index("tau")
    me = lax.axis_index("row")
    odd = lax.rem(me, 2)
    inner = me + 1 - 2 * odd
    outer = lax.rem(me - 1 + 2 * odd + row_count, row_count)
    share = rows // tau_count
    first = pl.multiple_of(tau * share, share)

    barrier = pltpu.get_barrier_semaphore()
    pl.semaphore_signal(barrier, inc=1, device_id={"row": inner}, device_id_type=MESH)
    pl.semaphore_signal(barrier, inc=1, device_id={"row": outer}, device_id_type=MESH)
    for step in range(1, tau_count):
        pl.semaphore_signal(
            barrier, inc=1, device_id={"tau": lax.rem(tau + step, tau_count)}, device_id_type=MESH
        )
    pl.semaphore_wait(barrier, tau_count + 1)

    outer_copies = {}
    for t in ORDER:
        copy = pltpu.make_async_remote_copy(
            src_ref=tiles_ref.at[4 * odd + t, pl.ds(first, share)],
            dst_ref=near.at[1, t, pl.ds(first, share)],
            send_sem=outer_send.at[t], recv_sem=outer_recv.at[t],
            device_id={"row": outer}, device_id_type=MESH,
        )
        copy.start()
        outer_copies[t] = copy
    own_copy = pltpu.make_async_copy(tiles_ref, own, own_sem)
    own_copy.start()
    inner_copies = []
    for t in range(NB_TILES):
        copy = pltpu.make_async_remote_copy(
            src_ref=tiles_ref.at[4 * (1 - odd) + t],
            dst_ref=near.at[0, t],
            send_sem=inner_send.at[t], recv_sem=inner_recv.at[t],
            device_id={"row": inner}, device_id_type=MESH,
        )
        copy.start()
        inner_copies.append(copy)

    fwd_copies = {t: [] for t in ORDER}

    def forward(t):
        outer_copies[t].wait_recv()
        for step in range(1, tau_count):
            place = near.at[1, t, pl.ds(first, share)]
            copy = pltpu.make_async_remote_copy(
                src_ref=place, dst_ref=place,
                send_sem=fwd_send.at[t, step - 1], recv_sem=fwd_recv.at[t, step - 1],
                device_id={"tau": lax.rem(tau + step, tau_count)}, device_id_type=MESH,
            )
            copy.start()
            fwd_copies[t].append(copy)

    left = lax.rem(me - 1 + row_count, row_count)
    right = lax.rem(me + 1, row_count)
    inner_kind = (1 - odd).astype(F32)
    outer_kind = odd.astype(F32)

    def flag(block, tile):
        return mask_ref[block, tile // 3, tile % 3].astype(F32)

    def setup():
        def spread(block):
            turned = block.T
            blank = jnp.zeros((width, width), F32)
            return jnp.concatenate([
                jnp.concatenate([turned, blank], axis=1),
                jnp.concatenate([blank, turned], axis=1),
            ], axis=0)

        before = spread(occ_ref[left, 2].astype(F32))
        middle = spread(occ_ref[me, 1].astype(F32))
        after = spread(occ_ref[right, 0].astype(F32))
        for o in range(3):
            for k, (matrix, tile) in enumerate(((before, 1 + o), (middle, 3 + o), (after, 5 + o))):
                weight_ref[k, o] = (matrix * flag(me, tile)).astype(BF16)
            for base, kind in ((3, inner_kind), (5, outer_kind)):
                other = 1.0 - kind
                first_right = kind * flag(right, o)
                second_right = kind * flag(right, 2 + o) if o > 0 else 0.0
                first_left = other * flag(left, 4 + o) if o < 2 else 0.0
                second_left = other * flag(left, 6 + o)
                weight_ref[base, o] = (middle * first_right + before * first_left).astype(BF16)
                weight_ref[base + 1, o] = (after * second_right + middle * second_left).astype(BF16)
        owners = (left, me, right)
        blank = jnp.zeros((width, width), F32)
        for a in range(3):
            virt_ref[a * width:(a + 1) * width, :] = jnp.concatenate([
                vir_ref[owners[a], b - a + 1].astype(F32) if 0 <= b - a + 1 < 3 else blank
                for b in range(3)
            ], axis=1).astype(BF16)

    def gate(slot, m):
        if slot == 0:
            return flag(me, 3 + m)
        kind = inner_kind if slot == 1 else outer_kind
        return kind * flag(right, m) + (1.0 - kind) * flag(left, 6 + m)

    def products(load, base, terms, bands=(0, 1, 2)):
        def at(step, carry):
            lane = pl.multiple_of(step * 256, 256)
            for o in bands:
                halves = []
                for half in range(2):
                    halves.append(jnp.concatenate(
                        [load(t, pl.ds(lane + 128 * half, 128)) for unused, t in terms[o]], axis=1))
                weight = jnp.concatenate([weight_ref[base + k, o] for k, unused in terms[o]], axis=1)
                result = lax.dot_general(
                    weight, jnp.concatenate(halves, axis=0), (((1,), (1,)), ((), ())),
                    preferred_element_type=F32)
                for q in range(4):
                    place = pl.ds(pl.multiple_of((4 * step + q) * pitch, 8), width)
                    prod[o, place, :] = result[
                        (q % 2) * width:(q % 2 + 1) * width, (q // 2) * rows:(q // 2 + 1) * rows]
            return carry

        lax.fori_loop(0, square // 256, at, 0, unroll=4)

    def virtual(block):
        def at(step, carry):
            columns = []
            for half in range(2):
                columns.append(jnp.concatenate(
                    [prod[m, pl.ds(2 * step + half, width, stride=pitch), :] for m in range(3)], axis=0))
            right = jnp.concatenate(columns, axis=1).astype(BF16)
            result = jnp.dot(virt_ref[...], right, preferred_element_type=F32)
            for half in range(2):
                for m in range(3):
                    part[m, pl.ds(2 * step + half, width, stride=pitch), :] = result[
                        m * width:(m + 1) * width, half * rows:(half + 1) * rows]
            return carry

        lax.fori_loop(0, width // 2, at, 0, unroll=8)

        def rounded(step, carry):
            place = pl.ds(pl.multiple_of(step * 512, 512), 512)
            for m in range(3):
                virt[m, place, block * rows:(block + 1) * rows] = jnp.concatenate([
                    part[m, pl.ds(pl.multiple_of((8 * step + q) * pitch, 8), width), :]
                    for q in range(8)
                ], axis=0).astype(BF16)
            return carry

        lax.fori_loop(0, square // 512, rounded, 0, unroll=2)

    def panel(load, slot, low, high, bands=(0, 1, 2), more=False):
        result = panels[slot, :, low * rows:high * rows] if more else None
        for m in bands:
            def at(step, carry, m=m):
                place = pl.ds(pl.multiple_of(step * 512, 512), 512)
                return carry + jnp.dot(
                    load(m, place), virt[m, place, low * rows:high * rows],
                    preferred_element_type=F32)

            term = lax.fori_loop(
                0, square // 512, at, jnp.zeros((rows, (high - low) * rows), F32), unroll=8)
            term = term * gate(slot, m)
            result = term if result is None else result + term
        panels[slot, :, low * rows:high * rows] = result

    def near_load(slot):
        return lambda t, lanes: near[slot, t, :, lanes]

    def near_partner(slot, offset):
        return lambda m, lanes: near[slot, offset + m, :, lanes]

    def own_load(t, lanes):
        return own[t, :, lanes]

    def own_partner(m, lanes):
        return own[3 + m, :, lanes]

    near_terms = tuple(((0, o), (1, 2 + o)) for o in range(3))

    def arrived(t):
        for copy in fwd_copies[t]:
            copy.wait_recv()

    places = (1, 2 * (1 - odd), 2 * odd)
    end_copies = []

    def finish(block, slot, target):
        sending[block - 1, slot] = panels[slot, :, block * rows:(block + 1) * rows].T
        copy = pltpu.make_async_remote_copy(
            src_ref=sending.at[block - 1, slot], dst_ref=arriving.at[block - 1, places[slot]],
            send_sem=end_send.at[block - 1, slot], recv_sem=end_recv.at[block - 1, slot],
            device_id={"row": target}, device_id_type=MESH,
        )
        copy.start()
        end_copies.append(copy)

    setup()
    own_copy.wait()
    products(own_load, 0, OWN_TERMS)
    virtual(0)
    forward(0)
    panel(own_partner, 0, 0, 1)
    for copy in inner_copies:
        copy.wait_recv()
    products(near_load(0), 3, near_terms)
    forward(2)
    virtual(1)
    panel(near_partner(0, 2 * odd), 1, 0, 2)
    panel(own_partner, 0, 1, 2)
    forward(1)
    arrived(0)
    arrived(2)
    products(near_load(1), 5, near_terms, (0,))
    forward(3)
    arrived(1)
    forward(4)
    arrived(3)
    products(near_load(1), 5, near_terms, (1,))
    panel(near_partner(1, 2 * (1 - odd)), 2, 0, 2, (0, 1))
    total[0] = jnp.zeros((rows, rows), F32)
    total[4] = jnp.zeros((rows, rows), F32)
    for slot in range(2):
        finish(1, slot, inner)
        total[1 + places[slot]] = panels[slot, :, :rows].T
    arrived(4)
    products(near_load(1), 5, near_terms, (2,))
    virtual(2)

    panel(own_partner, 0, 2, 3)
    finish(2, 0, outer)
    panel(near_partner(0, 2 * odd), 1, 2, 3)
    finish(2, 1, outer)
    panel(near_partner(1, 2 * (1 - odd)), 2, 2, 3)
    finish(2, 2, outer)
    panel(near_partner(1, 2 * (1 - odd)), 2, 0, 2, (2,), True)
    finish(1, 2, inner)
    total[1 + places[2]] = panels[2, :, :rows].T
    for copy in end_copies:
        copy.wait_recv()
    for index, place in ((0, 2 * (1 - odd)), (1, 2 * odd)):
        for k in range(3):
            total[place + k] += arriving[index, k]
    for c in range(5):
        out_ref[:, c * rows:(c + 1) * rows] = total[c] * -2.0
    for copy in list(outer_copies.values()) + inner_copies + end_copies:
        copy.wait_send()
    for group in fwd_copies.values():
        for copy in group:
            copy.wait_send()


def per_device(tau_count, row_count, integrals, occupied, virtual, tile_mask):
    rows, col_count, band_count, square = integrals.shape
    width = occupied.shape[-1]
    tiles = integrals.transpose(1, 2, 0, 3).reshape(col_count * band_count, rows, square)

    vmem = pl.BlockSpec(memory_space=pltpu.VMEM)
    dma = pltpu.SemaphoreType.DMA
    return pl.pallas_call(
        functools.partial(kernel, tau_count, row_count, width),
        out_shape=jax.ShapeDtypeStruct((rows, 5 * rows), F32),
        in_specs=[
            pl.BlockSpec(memory_space=pl.ANY), vmem, vmem,
            pl.BlockSpec(memory_space=pltpu.SMEM),
        ],
        out_specs=vmem,
        scratch_shapes=[
            pltpu.VMEM((7, 3, 2 * width, 2 * width), BF16),
            pltpu.VMEM((3 * width, 3 * width), BF16),
            pltpu.VMEM((9, rows, square), BF16),
            pltpu.VMEM((2, NB_TILES, rows, square), BF16),
            pltpu.VMEM((3, square + 8 * width, rows), F32),
            pltpu.VMEM((3, square + 8 * width, rows), F32),
            pltpu.VMEM((3, square, 3 * rows), BF16),
            pltpu.VMEM((3, rows, 3 * rows), F32),
            pltpu.VMEM((2, 3, rows, rows), F32),
            pltpu.VMEM((2, 3, rows, rows), F32),
            pltpu.VMEM((5, rows, rows), F32),
            dma, dma((NB_TILES,)), dma((NB_TILES,)), dma((NB_TILES,)), dma((NB_TILES,)),
            dma((NB_TILES, max(1, tau_count - 1))), dma((NB_TILES, max(1, tau_count - 1))),
            dma((2, 3)), dma((2, 3)),
        ],
        compiler_params=pltpu.CompilerParams(
            collective_id=0, has_side_effects=True, vmem_limit_bytes=56 * 1024 * 1024),
    )(tiles, occupied, virtual, tile_mask)


def solution(mesh):
    in_specs = (
        P("row", None, None, None),
        P("tau", None, None, None),
        P("tau", None, None, None),
        P(),
    )
    out_specs = P(("tau", "row"), None)
    return jax.shard_map(
        functools.partial(per_device, mesh.shape["tau"], mesh.shape["row"]),
        mesh=mesh, in_specs=in_specs, out_specs=out_specs, check_vma=False,
    )
```
